512 devices in a mesh: seq: 64 (over z, y_lo, core), head: 8 (over y_hi, x).
Axes of the slice: x: 4, y: 4 (y_hi: 2, y_lo: 2; y = y_hi * 2 + y_lo), z: 16, core: 2. Of those that a mesh axis runs over, the one named last changes fastest.
Arguments:
- query_rows: bfloat16 [16384, 4096], P('seq', 'head'), may hold values from -6 to 6
- key_rows: bfloat16 [16384, 1024], P('seq', 'head'), may hold values from -6 to 6
- value_rows: bfloat16 [16384, 1024], P('seq', 'head'), may hold values from -6 to 6
- out_weight: bfloat16 [4096, 4096], P('head'), may hold values from -0.125 to 0.125
- span_starts: int32 [64], replicated, may hold values from 0 to 16128, as said below
- round_masks: int32 [4], replicated, may hold values from 1 to 63, as said below
Outputs:
- projected: bfloat16 [16384, 4096], P('seq', 'head')
The draws below stay inside these ranges and needn't reach their ends.
Inputs may be any that keep to these rules, and one draw needn't show every extreme that they name: `span_starts`: each multiple of 256 below 16384 stands exactly once. `round_masks`: distinct values; the first equals 63.
All inputs are finite; a program needn't handle non-finite values.
Results may differ from the reference program's by a relative error of at most 0.017.
Values may be sent and summed in bfloat16 or wider, within the bound.
No kernel may reach another device: no remote copies, remote signals or barrier semaphores. Data moves between devices by JAX's collectives and lax.ppermute only.
A program may use at most 64 MiB of HBM per device.

```python
import jax
import jax.numpy as jnp
from jax import lax

HD = 128
KVH = 8
GROUP = 4
DOUT = 4096
TOK_DEV = 256
ROUNDS = 4
HQ = 32
TOKENS = 16384
SHARE_ROWS = 512
N_SEQ = 64
N_HEAD = 8


def draw_query_rows(key, part):
    width = HQ * HD
    base = jnp.clip(2.0 * jax.random.normal(jax.random.fold_in(key, 11), (TOKENS, width), jnp.float32), -6.0, 6.0)
    return base.astype(jnp.bfloat16)


def draw_key_rows(key, part):
    width = KVH * HD
    base = jnp.clip(jax.random.normal(jax.random.fold_in(key, 12), (TOKENS, width), jnp.float32), -6.0, 6.0)
    return base.astype(jnp.bfloat16)


def draw_span_starts(key, part):
    spans = TOKENS // TOK_DEV
    order_drawn = jax.random.permutation(jax.random.fold_in(key, 21), spans)
    return (order_drawn * TOK_DEV).astype(jnp.int32)


def draw_round_masks(key, part):
    spans = TOKENS // TOK_DEV
    others = jax.random.permutation(jax.random.fold_in(key, 22), spans - 2)[:ROUNDS - 1] + 1
    leading = jnp.full((1,), spans - 1, jnp.int32)
    return jnp.concatenate([leading, others.astype(jnp.int32)]).astype(jnp.int32)


def spiked(entries, rng, source, target, shards_of, factor):
    owner, partner = [(jnp.arange(entries.shape[axis_at]) // (entries.shape[axis_at] // shards_of)).reshape([-1 if axis == axis_at else 1 for axis in range(entries.ndim)]) for axis_at in (source, target)]
    chosen = jax.random.permutation(rng, shards_of)[partner]
    strong = (owner == chosen) | (owner == (partner + shards_of // 2) % shards_of)
    return jnp.where(strong, factor * entries, entries)


def level_of(key, extent, cuts, smallest, high):
    level, own = 1.0, jax.random.fold_in(key, 6)
    for axis_at, parts in cuts:
        heights = jnp.exp(jax.random.uniform(jax.random.fold_in(own, axis_at), (parts,), jnp.float32, smallest / len(cuts), high / len(cuts)))
        level = level * jnp.repeat(heights, extent[axis_at] // parts).reshape([-1 if axis == axis_at else 1 for axis in range(len(extent))])
    return level


def normal_values(stream_key, extent, deviation, reach, split=(), held_as=jnp.bfloat16):
    values = jax.random.normal(stream_key, extent, jnp.float32) * deviation
    if len(split) > 0:
        values = level_of(stream_key, extent, split, -0.22, 0.18) * values
    return jnp.clip(values, min=-reach, max=reach).astype(held_as)


def heavy_noise(key, shape, scale, reach, split, heavy, held_as=jnp.bfloat16):
    values = scale * jax.random.normal(key, shape, jnp.float32)
    if split:
        values = values * level_of(key, shape, split, -0.22, 0.18)
    return jnp.clip(spiked(values, jax.random.fold_in(key, 3), *heavy), -reach, reach).astype(held_as)


def setup_inputs(seed: int = 0) -> dict:
    keys = jax.random.split(jax.random.key(seed), 7)
    return {
        "query_rows": draw_query_rows(jax.random.fold_in(keys[6], 71), 0),
        "key_rows": draw_key_rows(jax.random.fold_in(keys[6], 71), 0),
        "value_rows": normal_values(keys[2], (TOKENS, KVH * HD), 1.0, 6.0, ((0, 64), (1, 8))),
        "out_weight": heavy_noise(keys[3], (HQ * HD, DOUT), (HQ * HD) ** -0.5, 0.125, ((0, 8),), (0, 1, 8, 2.0)),
        "span_starts": draw_span_starts(jax.random.fold_in(keys[6], 71), 0),
        "round_masks": draw_round_masks(jax.random.fold_in(keys[6], 71), 0),
    }


def reference(query_rows, key_rows, value_rows, out_weight, span_starts, round_masks):
    score_scale = HD ** -0.5
    query_spans = query_rows.reshape(N_SEQ, TOK_DEV, KVH, GROUP, HD)
    key_spans = key_rows.reshape(N_SEQ, TOK_DEV, KVH, HD)
    value_spans = value_rows.reshape(N_SEQ, TOK_DEV, KVH, HD)
    offsets = jnp.arange(TOK_DEV, dtype=jnp.int32)

    def one_span(span_id):
        partners = jnp.concatenate([span_id[None], jnp.bitwise_xor(span_id, round_masks)]).astype(jnp.int32)
        seen_keys = key_spans[partners].reshape(-1, KVH, HD).astype(jnp.float32)
        seen_values = value_spans[partners].reshape(-1, KVH, HD).astype(jnp.float32)
        key_pos = (span_starts[partners][:, None] + offsets[None, :]).reshape(-1)
        query_pos = span_starts[span_id] + offsets
        query_here = query_spans[span_id].astype(jnp.float32)
        scores = jnp.einsum("tkgd,skd->kgts", query_here, seen_keys) * score_scale
        allowed = key_pos[None, :] <= query_pos[:, None]
        scores = jnp.where(allowed, scores, -jnp.inf)
        row_peak = jnp.max(scores, axis=-1, keepdims=True)
        weights = jnp.exp(scores - row_peak)
        row_total = jnp.sum(weights, axis=-1)
        rounded = lax.optimization_barrier(weights.astype(jnp.bfloat16)).astype(jnp.float32)
        summed = jnp.einsum("kgts,skd->kgtd", rounded, seen_values)
        result = summed / row_total[..., None]
        return jnp.transpose(result, (2, 0, 1, 3)).reshape(TOK_DEV, KVH * GROUP * HD).astype(jnp.bfloat16)

    attended = lax.map(one_span, jnp.arange(N_SEQ, dtype=jnp.int32)).reshape(TOKENS, KVH * GROUP * HD)

    def add_share(running, group_id):
        begin = (group_id * SHARE_ROWS).astype(jnp.int32)
        attended_part = lax.dynamic_slice_in_dim(attended, begin, SHARE_ROWS, 1)
        weight_part = lax.dynamic_slice_in_dim(out_weight, begin, SHARE_ROWS, 0)
        product = jnp.dot(attended_part, weight_part, preferred_element_type=jnp.float32)
        rounded = lax.optimization_barrier(product.astype(jnp.bfloat16)).astype(jnp.float32)
        return running + rounded, None

    projected, _ = lax.scan(add_share, jnp.zeros((TOKENS, DOUT), jnp.float32), jnp.arange(N_HEAD, dtype=jnp.int32))
    return projected.astype(jnp.bfloat16)
```

```python
import jax
import jax.numpy as jnp
from jax import lax
from jax.experimental import pallas as pl
from jax.experimental.pallas import tpu as pltpu
from jax.sharding import PartitionSpec as P

HD = 128
GROUP = 4
FAR_BELOW = -1e30
LOG2E = 1.4426950408889634


def attend_project(starts_ref, masks_ref, q_ref, kv_ref, f0, f1, f2, f3, w_ref, out_ref, peak, total, summed, attended):
    span = q_ref.shape[0]
    me = lax.axis_index("seq")
    own_start = starts_ref[me]

    def update(block, first, causal):
        keys = block[0:span, :]
        values = block[span : 2 * span, :]
        for h in range(GROUP):
            cols = slice(h * HD, (h + 1) * HD)
            scores = lax.dot_general(
                q_ref[:, cols], keys, (((1,), (1,)), ((), ())), preferred_element_type=jnp.float32
            ) * (HD ** (-0.5) * LOG2E)
            if causal:
                row = lax.broadcasted_iota(jnp.int32, scores.shape, 0)
                col = lax.broadcasted_iota(jnp.int32, scores.shape, 1)
                scores = jnp.where(col <= row, scores, FAR_BELOW)
            block_peak = jnp.max(scores, axis=1, keepdims=True)
            if first:
                new_peak = block_peak
            else:
                old_peak = peak[h, :, 0:1]
                new_peak = jnp.maximum(old_peak, block_peak)
            weights = jnp.exp2(scores - new_peak)
            block_total = jnp.sum(weights, axis=1, keepdims=True)
            block_sum = jnp.dot(weights.astype(jnp.bfloat16), values, preferred_element_type=jnp.float32)
            if not first:
                lift = jnp.exp2(old_peak - new_peak)
                block_total = block_total + total[h, :, 0:1] * lift
                block_sum = block_sum + summed[:, cols] * lift
            peak[h] = jnp.broadcast_to(new_peak, (span, HD))
            total[h] = jnp.broadcast_to(block_total, (span, HD))
            summed[:, cols] = block_sum

    @pl.when(pl.program_id(0) == 0)
    def _():
        update(kv_ref, True, True)
        for r, far in enumerate((f0, f1, f2, f3)):
            partner = jnp.bitwise_xor(me, masks_ref[r])

            @pl.when(starts_ref[partner] < own_start)
            def _(far=far):
                update(far, False, False)

        for h in range(GROUP):
            cols = slice(h * HD, (h + 1) * HD)
            attended[:, cols] = (summed[:, cols] / total[h]).astype(jnp.bfloat16)

    out_ref[0] = jnp.dot(attended[...], w_ref[...], preferred_element_type=jnp.float32).astype(jnp.bfloat16)


def add_shares(got_ref, out_ref):
    acc = got_ref[0].astype(jnp.float32)
    for j in range(1, got_ref.shape[0]):
        acc = acc + got_ref[j].astype(jnp.float32)
    out_ref[...] = acc.astype(out_ref.dtype)


def permuted(mask):
    return lambda x: lax.ppermute(x, "seq", [(i, i ^ mask) for i in range(lax.axis_size("seq"))])


def per_device(query_rows, key_rows, value_rows, out_weight, span_starts, round_masks):
    span, width = query_rows.shape
    heads = lax.axis_size("head")
    spans = lax.axis_size("seq")
    dout = out_weight.shape[1]
    cut = dout // heads
    kv = jnp.concatenate([key_rows, value_rows], axis=0)
    fars = [permuted(spans - 1)(kv)]
    for r in range(1, round_masks.shape[0]):
        fars.append(lax.switch(round_masks[r] - 1, [permuted(k) for k in range(1, spans - 1)], kv))

    whole = lambda shape: pl.BlockSpec(shape, lambda j, *_: (0,) * len(shape))
    shares = pl.pallas_call(
        attend_project,
        grid_spec=pltpu.PrefetchScalarGridSpec(
            num_scalar_prefetch=2,
            grid=(heads,),
            in_specs=[whole((span, width))]
            + [whole((2 * span, HD))] * 5
            + [pl.BlockSpec((width, cut), lambda j, *_: (0, j))],
            out_specs=pl.BlockSpec((1, span, cut), lambda j, *_: (j, 0, 0)),
            scratch_shapes=[
                pltpu.VMEM((GROUP, span, HD), jnp.float32),
                pltpu.VMEM((GROUP, span, HD), jnp.float32),
                pltpu.VMEM((span, width), jnp.float32),
                pltpu.VMEM((span, width), jnp.bfloat16),
            ],
        ),
        out_shape=jax.ShapeDtypeStruct((heads, span, cut), jnp.bfloat16),
        compiler_params=pltpu.CompilerParams(vmem_limit_bytes=32 * 2**20),
        cost_estimate=pl.CostEstimate(flops=3 * 2**30, bytes_accessed=8 * 2**20, transcendentals=2**21),
        name="attend_project",
    )(span_starts, round_masks, query_rows, kv, *fars, out_weight)
    got = lax.all_to_all(shares, "head", 0, 0, tiled=True)
    return pl.pallas_call(
        add_shares,
        grid=(4,),
        in_specs=[pl.BlockSpec((heads, span // 4, cut), lambda j: (0, j, 0))],
        out_specs=pl.BlockSpec((span // 4, cut), lambda j: (j, 0)),
        out_shape=jax.ShapeDtypeStruct((span, cut), jnp.bfloat16),
        compiler_params=pltpu.CompilerParams(vmem_limit_bytes=32 * 2**20),
        name="add_shares",
    )(got)


def solution(mesh):
    in_specs = (P("seq", "head"), P("seq", "head"), P("seq", "head"), P("head", None), P(), P())
    out_specs = P("seq", "head")
    return jax.shard_map(
        per_device, mesh=mesh, in_specs=in_specs, out_specs=out_specs, check_vma=False
    )
```

```python
import jax
import jax.numpy as jnp
from jax import lax
from jax.experimental import pallas as pl
from jax.experimental.pallas import tpu as pltpu
from jax.sharding import Mesh, PartitionSpec as P

HD = 128
GROUP = 4
FAR_BELOW = -1e30
LOG2E = 1.4426950408889634


def attend_project(starts_ref, masks_ref, q_ref, kv_ref, f0, f1, f2, f3, w_ref, out_ref, peak, total, summed, attended):
    span = q_ref.shape[0]
    me = lax.axis_index(("chip", "core"))
    own_start = starts_ref[me]

    def update(block, first, causal):
        keys = block[0:span, :]
        values = block[span : 2 * span, :]
        for h in range(GROUP):
            cols = slice(h * HD, (h + 1) * HD)
            scores = lax.dot_general(
                q_ref[:, cols], keys, (((1,), (1,)), ((), ())), preferred_element_type=jnp.float32
            ) * (HD ** (-0.5) * LOG2E)
            if causal:
                row = lax.broadcasted_iota(jnp.int32, scores.shape, 0)
                col = lax.broadcasted_iota(jnp.int32, scores.shape, 1)
                scores = jnp.where(col <= row, scores, FAR_BELOW)
            block_peak = jnp.max(scores, axis=1, keepdims=True)
            if first:
                new_peak = block_peak
            else:
                old_peak = peak[h, :, 0:1]
                new_peak = jnp.maximum(old_peak, block_peak)
            weights = jnp.exp2(scores - new_peak)
            block_total = jnp.sum(weights, axis=1, keepdims=True)
            block_sum = jnp.dot(weights.astype(jnp.bfloat16), values, preferred_element_type=jnp.float32)
            if not first:
                lift = jnp.exp2(old_peak - new_peak)
                block_total = block_total + total[h, :, 0:1] * lift
                block_sum = block_sum + summed[:, cols] * lift
            peak[h] = jnp.broadcast_to(new_peak, (span, HD))
            total[h] = jnp.broadcast_to(block_total, (span, HD))
            summed[:, cols] = block_sum

    @pl.when(pl.program_id(0) == 0)
    def _():
        update(kv_ref, True, True)
        for r, far in enumerate((f0, f1, f2, f3)):
            partner = jnp.bitwise_xor(me, masks_ref[r])

            @pl.when(starts_ref[partner] < own_start)
            def _(far=far):
                update(far, False, False)

        for h in range(GROUP):
            cols = slice(h * HD, (h + 1) * HD)
            attended[:, cols] = (summed[:, cols] / total[h]).astype(jnp.bfloat16)

    out_ref[0] = jnp.dot(attended[...], w_ref[...], preferred_element_type=jnp.float32).astype(jnp.bfloat16)


def add_shares(got_ref, out_ref):
    acc = got_ref[0].astype(jnp.float32)
    for j in range(1, got_ref.shape[0]):
        acc = acc + got_ref[j].astype(jnp.float32)
    out_ref[...] = acc.astype(out_ref.dtype)


def stack_rows(key_ref, value_ref, out_ref):
    span = key_ref.shape[0]
    out_ref[0:span, :] = key_ref[...]
    out_ref[span:, :] = value_ref[...]


def pick_core(masks_ref, both_ref, *out_refs):
    rows = out_refs[0].shape[0]
    me = lax.axis_index("core")
    for r, out_ref in enumerate(out_refs):
        source = jnp.bitwise_xor(me, jnp.bitwise_and(masks_ref[r], 1))
        out_ref[...] = both_ref[pl.ds(pl.multiple_of(source * rows, rows), rows), :]


def swapped(mask):
    if mask == 0:
        return lambda x: x
    return lambda x: lax.ppermute(x, "chip", [(i, i ^ mask) for i in range(lax.axis_size("chip"))])


def per_device(query_rows, key_rows, value_rows, out_weight, span_starts, round_masks):
    span, width = query_rows.shape
    heads = lax.axis_size("head")
    chips = lax.axis_size("chip")
    rounds = round_masks.shape[0]
    dout = out_weight.shape[1]
    cut = dout // heads
    pair = jax.ShapeDtypeStruct((2 * span, HD), jnp.bfloat16)
    kv = pl.pallas_call(stack_rows, out_shape=pair, name="stack_rows")(key_rows, value_rows)
    both = lax.all_gather(kv, "core", tiled=True)
    sends = pl.pallas_call(
        pick_core,
        grid_spec=pltpu.PrefetchScalarGridSpec(
            num_scalar_prefetch=1,
            grid=(1,),
            in_specs=[pl.BlockSpec((4 * span, HD), lambda i, _: (0, 0))],
            out_specs=[pl.BlockSpec((2 * span, HD), lambda i, _: (0, 0))] * rounds,
        ),
        out_shape=[pair] * rounds,
        name="pick_core",
    )(round_masks, both)
    fars = [swapped(chips - 1)(sends[0])]
    for r in range(1, rounds):
        fars.append(lax.switch(round_masks[r] >> 1, [swapped(k) for k in range(chips)], sends[r]))

    whole = lambda shape: pl.BlockSpec(shape, lambda j, *_: (0,) * len(shape))
    shares = pl.pallas_call(
        attend_project,
        grid_spec=pltpu.PrefetchScalarGridSpec(
            num_scalar_prefetch=2,
            grid=(heads,),
            in_specs=[whole((span, width))]
            + [whole((2 * span, HD))] * 5
            + [pl.BlockSpec((width, cut), lambda j, *_: (0, j))],
            out_specs=pl.BlockSpec((1, span, cut), lambda j, *_: (j, 0, 0)),
            scratch_shapes=[
                pltpu.VMEM((GROUP, span, HD), jnp.float32),
                pltpu.VMEM((GROUP, span, HD), jnp.float32),
                pltpu.VMEM((span, width), jnp.float32),
                pltpu.VMEM((span, width), jnp.bfloat16),
            ],
        ),
        out_shape=jax.ShapeDtypeStruct((heads, span, cut), jnp.bfloat16),
        compiler_params=pltpu.CompilerParams(vmem_limit_bytes=58 * 2**20),
        cost_estimate=pl.CostEstimate(flops=3 * 2**30, bytes_accessed=8 * 2**20, transcendentals=2**21),
        name="attend_project",
    )(span_starts, round_masks, query_rows, kv, *fars, out_weight)
    got = lax.all_to_all(shares, "head", 0, 0, tiled=True)
    return pl.pallas_call(
        add_shares,
        grid=(4,),
        in_specs=[pl.BlockSpec((heads, span // 4, cut), lambda j: (0, j, 0))],
        out_specs=pl.BlockSpec((span // 4, cut), lambda j: (j, 0)),
        out_shape=jax.ShapeDtypeStruct((span, cut), jnp.bfloat16),
        compiler_params=pltpu.CompilerParams(vmem_limit_bytes=32 * 2**20),
        name="add_shares",
    )(got)


def solution(mesh):
    seq, head = mesh.devices.shape
    fine = Mesh(mesh.devices.reshape(seq // 2, 2, head), ("chip", "core", "head"))
    rows = ("chip", "core")
    in_specs = (P(rows, "head"), P(rows, "head"), P(rows, "head"), P("head", None), P(), P())
    return jax.shard_map(
        per_device, mesh=fine, in_specs=in_specs, out_specs=P(rows, "head"), check_vma=False
    )
```

```python
import jax
import jax.numpy as jnp
from jax import lax
from jax.experimental import pallas as pl
from jax.experimental.pallas import tpu as pltpu
from jax.sharding import Mesh, PartitionSpec as P

HD = 128
GROUP = 4
FAR_BELOW = -1e30
SCALE = HD ** (-0.5) * 1.4426950408889634


def attend_project(
    starts_ref, masks_ref, q_ref, kv_ref, f0, f1, f2, f3, w_hbm, out_hbm, attended, w_ref, out_ref, w_sem, out_sem
):
    span = q_ref.shape[0]
    parts, _, cut = out_ref.shape
    w_copies = [
        pltpu.make_async_copy(w_hbm.at[:, pl.ds(j * cut, cut)], w_ref.at[j], w_sem.at[j]) for j in range(parts)
    ]
    for copy in w_copies:
        copy.start()
    me = lax.axis_index(("chip", "core"))
    own_start = starts_ref[me]
    blocks = [kv_ref, f0, f1, f2, f3]
    hidden = [0.0]
    for r in range(len(blocks) - 1):
        partner = jnp.bitwise_xor(me, masks_ref[r])
        hidden.append(jnp.where(starts_ref[partner] < own_start, 0.0, -FAR_BELOW))
    key = lax.broadcasted_iota(jnp.int32, (span, span), 0)
    token = lax.broadcasted_iota(jnp.int32, (span, span), 1)
    for h in range(GROUP):
        q = q_ref[:, h * HD : (h + 1) * HD]
        scores, peak = [], None
        for b, block in enumerate(blocks):
            part = lax.dot_general(
                block[0:span, :], q, (((1,), (1,)), ((), ())), preferred_element_type=jnp.float32
            )
            if b == 0:
                part = jnp.where(key <= token, part, FAR_BELOW)
            part_peak = jnp.max(part, axis=0, keepdims=True) * SCALE - hidden[b]
            peak = part_peak if b == 0 else jnp.maximum(peak, part_peak)
            scores.append(part)
        total, summed = 0.0, 0.0
        for b, block in enumerate(blocks):
            weights = jnp.exp2(scores[b] * SCALE - (peak + hidden[b]))
            total = total + jnp.sum(weights, axis=0, keepdims=True)
            summed = summed + lax.dot_general(
                block[span : 2 * span, :],
                weights.astype(jnp.bfloat16),
                (((0,), (0,)), ((), ())),
                preferred_element_type=jnp.float32,
            )
        attended[:, h * HD : (h + 1) * HD] = jnp.transpose(summed / total).astype(jnp.bfloat16)
    out_copies = []
    for j in range(parts):
        w_copies[j].wait()
        out_ref[j] = jnp.dot(attended[...], w_ref[j], preferred_element_type=jnp.float32).astype(jnp.bfloat16)
        out_copies.append(pltpu.make_async_copy(out_ref.at[j], out_hbm.at[j], out_sem.at[j]))
        out_copies[j].start()
    for copy in out_copies:
        copy.wait()


def add_shares(got_ref, out_ref):
    acc = got_ref[0].astype(jnp.float32)
    for j in range(1, got_ref.shape[0]):
        acc = acc + got_ref[j].astype(jnp.float32)
    out_ref[...] = acc.astype(out_ref.dtype)


def stack_rows(key_ref, value_ref, out_ref):
    span = key_ref.shape[0]
    out_ref[0:span, :] = key_ref[...]
    out_ref[span:, :] = value_ref[...]


def sent(mask):
    def send(own, other):
        block = other if mask & 1 else own
        if mask >> 1 == 0:
            return block
        return lax.ppermute(block, "chip", [(i, i ^ (mask >> 1)) for i in range(lax.axis_size("chip"))])

    return send


def per_device(query_rows, key_rows, value_rows, out_weight, span_starts, round_masks):
    span, width = query_rows.shape
    heads = lax.axis_size("head")
    spans = 2 * lax.axis_size("chip")
    cut = out_weight.shape[1] // heads
    kv = pl.pallas_call(
        stack_rows, out_shape=jax.ShapeDtypeStruct((2 * span, HD), jnp.bfloat16), name="stack_rows"
    )(key_rows, value_rows)
    other = lax.ppermute(kv, "core", [(0, 1), (1, 0)])
    fars = [sent(spans - 1)(kv, other)]
    for r in range(1, round_masks.shape[0]):
        fars.append(lax.switch(round_masks[r], [sent(k) for k in range(spans)], kv, other))

    vmem = pl.BlockSpec(memory_space=pltpu.VMEM)
    smem = pl.BlockSpec(memory_space=pltpu.SMEM)
    anywhere = pl.BlockSpec(memory_space=pl.ANY)
    shares = pl.pallas_call(
        attend_project,
        in_specs=[smem] * 2 + [vmem] * 6 + [anywhere],
        out_specs=anywhere,
        out_shape=jax.ShapeDtypeStruct((heads, span, cut), jnp.bfloat16),
        scratch_shapes=[
            pltpu.VMEM((span, width), jnp.bfloat16),
            pltpu.VMEM((heads, width, cut), jnp.bfloat16),
            pltpu.VMEM((heads, span, cut), jnp.bfloat16),
            pltpu.SemaphoreType.DMA((heads,)),
            pltpu.SemaphoreType.DMA((heads,)),
        ],
        compiler_params=pltpu.CompilerParams(vmem_limit_bytes=56 * 2**20),
        cost_estimate=pl.CostEstimate(flops=3 * 2**30, bytes_accessed=8 * 2**20, transcendentals=2**21),
        name="attend_project",
    )(span_starts, round_masks, query_rows, kv, *fars, out_weight)
    got = lax.all_to_all(shares, "head", 0, 0, tiled=True)
    return pl.pallas_call(
        add_shares,
        grid=(4,),
        in_specs=[pl.BlockSpec((heads, span // 4, cut), lambda j: (0, j, 0))],
        out_specs=pl.BlockSpec((span // 4, cut), lambda j: (j, 0)),
        out_shape=jax.ShapeDtypeStruct((span, cut), jnp.bfloat16),
        compiler_params=pltpu.CompilerParams(vmem_limit_bytes=32 * 2**20),
        name="add_shares",
    )(got)


def solution(mesh):
    seq, head = mesh.devices.shape
    fine = Mesh(mesh.devices.reshape(seq // 2, 2, head), ("chip", "core", "head"))
    rows = ("chip", "core")
    in_specs = (P(rows, "head"), P(rows, "head"), P(rows, "head"), P("head", None), P(), P())
    return jax.shard_map(
        per_device, mesh=fine, in_specs=in_specs, out_specs=P(rows, "head"), check_vma=False
    )
```

```python
import jax
import jax.numpy as jnp
from jax import lax
from jax.experimental import pallas as pl
from jax.experimental.pallas import tpu as pltpu
from jax.sharding import Mesh, PartitionSpec as P

HD = 128
GROUP = 4
FAR_BELOW = -1e30
SCALE = HD ** (-0.5) * 1.4426950408889634


def in_order(masks):
    a, b, c = masks[1], masks[2], masks[3]
    low = jnp.minimum(jnp.minimum(a, b), c)
    high = jnp.maximum(jnp.maximum(a, b), c)
    return low, a + b + c - low - high, high


def attend_project(
    starts_ref, masks_ref, q_ref, kv_ref, f0, f1, f2, f3, w_hbm, out_hbm, attended, w_ref, out_ref, w_sem, out_sem
):
    span = q_ref.shape[0]
    parts, _, cut = out_ref.shape
    w_copies = [
        pltpu.make_async_copy(w_hbm.at[:, pl.ds(j * cut, cut)], w_ref.at[j], w_sem.at[j]) for j in range(parts)
    ]
    for copy in w_copies:
        copy.start()
    me = lax.axis_index(("chip", "core"))
    own_start = starts_ref[me]
    blocks = [kv_ref, f0, f1, f2, f3]
    hidden = [0.0]
    for mask in (masks_ref[0], *in_order(masks_ref)):
        partner = jnp.bitwise_xor(me, mask)
        hidden.append(jnp.where(starts_ref[partner] < own_start, 0.0, -FAR_BELOW))
    key = lax.broadcasted_iota(jnp.int32, (span, span), 0)
    token = lax.broadcasted_iota(jnp.int32, (span, span), 1)
    for h in range(GROUP):
        q = q_ref[:, h * HD : (h + 1) * HD]
        scores, peak = [], None
        for b, block in enumerate(blocks):
            part = lax.dot_general(
                block[0:span, :], q, (((1,), (1,)), ((), ())), preferred_element_type=jnp.float32
            )
            if b == 0:
                part = jnp.where(key <= token, part, FAR_BELOW)
            part_peak = jnp.max(part, axis=0, keepdims=True) * SCALE - hidden[b]
            peak = part_peak if b == 0 else jnp.maximum(peak, part_peak)
            scores.append(part)
        total, summed = 0.0, 0.0
        for b, block in enumerate(blocks):
            weights = jnp.exp2(scores[b] * SCALE - (peak + hidden[b]))
            total = total + jnp.sum(weights, axis=0, keepdims=True)
            summed = summed + lax.dot_general(
                block[span : 2 * span, :],
                weights.astype(jnp.bfloat16),
                (((0,), (0,)), ((), ())),
                preferred_element_type=jnp.float32,
            )
        attended[:, h * HD : (h + 1) * HD] = jnp.transpose(summed / total).astype(jnp.bfloat16)
    out_copies = []
    for j in range(parts):
        w_copies[j].wait()
        out_ref[j] = jnp.dot(attended[...], w_ref[j], preferred_element_type=jnp.float32).astype(jnp.bfloat16)
        out_copies.append(pltpu.make_async_copy(out_ref.at[j], out_hbm.at[j], out_sem.at[j]))
        out_copies[j].start()
    for copy in out_copies:
        copy.wait()


def add_shares(got_ref, out_ref):
    acc = got_ref[0].astype(jnp.float32)
    for j in range(1, got_ref.shape[0]):
        acc = acc + got_ref[j].astype(jnp.float32)
    out_ref[...] = acc.astype(out_ref.dtype)


def prepare(masks_ref, key_ref, value_ref, kv_ref, low_ref, middle_ref, high_ref):
    span = key_ref.shape[0]
    low_ref[0], middle_ref[0], high_ref[0] = in_order(masks_ref)
    kv_ref[0:span, :] = key_ref[...]
    kv_ref[span:, :] = value_ref[...]


def across_chips(block, mask):
    if mask == 0:
        return block
    return lax.ppermute(block, "chip", [(i, i ^ mask) for i in range(lax.axis_size("chip"))])


def across_cores(block):
    return lax.ppermute(block, "core", [(0, 1), (1, 0)])


def direct(mask):
    return lambda own, other, *_: across_chips(other if mask & 1 else own, mask >> 1)


def by_mirror(mask, last):
    rest = mask ^ last

    def fetch(own, other, mirrored):
        block = across_cores(mirrored) if rest & 1 else mirrored
        return across_chips(block, rest >> 1)

    return fetch


def nearer(mask, spans):
    if mask & 1:
        return mask >= spans * 11 // 16 or spans // 2 <= mask < spans * 5 // 8
    return mask >= spans * 7 // 8


def per_device(query_rows, key_rows, value_rows, out_weight, span_starts, round_masks):
    span, width = query_rows.shape
    heads = lax.axis_size("head")
    spans = 2 * lax.axis_size("chip")
    cut = out_weight.shape[1] // heads
    vmem = pl.BlockSpec(memory_space=pltpu.VMEM)
    smem = pl.BlockSpec(memory_space=pltpu.SMEM)
    anywhere = pl.BlockSpec(memory_space=pl.ANY)
    scalar = jax.ShapeDtypeStruct((1,), jnp.int32)
    kv, low, middle, high = pl.pallas_call(
        prepare,
        in_specs=[smem, vmem, vmem],
        out_specs=[vmem, smem, smem, smem],
        out_shape=[jax.ShapeDtypeStruct((2 * span, HD), jnp.bfloat16), scalar, scalar, scalar],
        name="prepare",
    )(round_masks, key_rows, value_rows)
    last = spans - 1
    mirrored = lax.ppermute(kv, ("chip", "core"), [(i, i ^ last) for i in range(spans)])
    other = across_cores(kv)
    plain = [direct(k) for k in range(spans)]
    mixed = [by_mirror(k, last) if nearer(k, spans) else direct(k) for k in range(spans)]
    first = lax.switch(low[0], plain, kv, other)
    second = lax.switch(middle[0], mixed, kv, other, mirrored)
    third = lax.switch(high[0], mixed, kv, other, mirrored)
    fars = (mirrored, first, second, third)
    shares = pl.pallas_call(
        attend_project,
        in_specs=[smem] * 2 + [vmem] * 6 + [anywhere],
        out_specs=anywhere,
        out_shape=jax.ShapeDtypeStruct((heads, span, cut), jnp.bfloat16),
        scratch_shapes=[
            pltpu.VMEM((span, width), jnp.bfloat16),
            pltpu.VMEM((heads, width, cut), jnp.bfloat16),
            pltpu.VMEM((heads, span, cut), jnp.bfloat16),
            pltpu.SemaphoreType.DMA((heads,)),
            pltpu.SemaphoreType.DMA((heads,)),
        ],
        compiler_params=pltpu.CompilerParams(vmem_limit_bytes=56 * 2**20),
        cost_estimate=pl.CostEstimate(flops=3 * 2**30, bytes_accessed=8 * 2**20, transcendentals=2**21),
        name="attend_project",
    )(span_starts, round_masks, query_rows, kv, *fars, out_weight)
    got = lax.all_to_all(shares, "head", 0, 0, tiled=True)
    return pl.pallas_call(
        add_shares,
        grid=(4,),
        in_specs=[pl.BlockSpec((heads, span // 4, cut), lambda j: (0, j, 0))],
        out_specs=pl.BlockSpec((span // 4, cut), lambda j: (j, 0)),
        out_shape=jax.ShapeDtypeStruct((span, cut), jnp.bfloat16),
        compiler_params=pltpu.CompilerParams(vmem_limit_bytes=32 * 2**20),
        name="add_shares",
    )(got)


def solution(mesh):
    seq, head = mesh.devices.shape
    fine = Mesh(mesh.devices.reshape(seq // 2, 2, head), ("chip", "core", "head"))
    rows = ("chip", "core")
    in_specs = (P(rows, "head"), P(rows, "head"), P(rows, "head"), P("head", None), P(), P())
    return jax.shard_map(
        per_device, mesh=fine, in_specs=in_specs, out_specs=P(rows, "head"), check_vma=False
    )
```

```python
import functools

import jax
import jax.numpy as jnp
from jax import lax
from jax.experimental import pallas as pl
from jax.experimental.pallas import tpu as pltpu
from jax.sharding import Mesh, PartitionSpec as P

HD = 128
GROUP = 4
FAR_BELOW = -1e30
SCALE = HD ** (-0.5) * 1.4426950408889634


def in_order(masks):
    a, b, c = masks[1], masks[2], masks[3]
    low = jnp.minimum(jnp.minimum(a, b), c)
    high = jnp.maximum(jnp.maximum(a, b), c)
    return low, a + b + c - low - high, high


def attend_project(
    starts_ref, masks_ref, q_ref, kv_ref, f0, f1, f2, f3, w_hbm, out_hbm, attended, w_ref, out_ref, w_sem, out_sem
):
    span = q_ref.shape[0]
    parts, _, cut = out_ref.shape
    w_copies = [
        pltpu.make_async_copy(w_hbm.at[:, pl.ds(j * cut, cut)], w_ref.at[j], w_sem.at[j]) for j in range(parts)
    ]
    for copy in w_copies:
        copy.start()
    me = lax.axis_index(("chip", "core"))
    own_start = starts_ref[me]
    blocks = [kv_ref, f0, f1, f2, f3]
    hidden = [0.0]
    for mask in (masks_ref[0], *in_order(masks_ref)):
        partner = jnp.bitwise_xor(me, mask)
        hidden.append(jnp.where(starts_ref[partner] < own_start, 0.0, -FAR_BELOW))
    key = lax.broadcasted_iota(jnp.int32, (span, span), 0)
    token = lax.broadcasted_iota(jnp.int32, (span, span), 1)

    def score(h):
        q = q_ref[:, h * HD : (h + 1) * HD]
        scores, peak = [], None
        for b, block in enumerate(blocks):
            part = lax.dot_general(
                block[0:span, :], q, (((1,), (1,)), ((), ())), preferred_element_type=jnp.float32
            )
            if b == 0:
                part = jnp.where(key <= token, part, FAR_BELOW)
            part_peak = jnp.max(part, axis=0, keepdims=True) * SCALE - hidden[b]
            peak = part_peak if b == 0 else jnp.maximum(peak, part_peak)
            scores.append(part)
        return scores, peak

    ahead = score(0)
    for h in range(GROUP):
        scores, peak = ahead
        ahead = score(h + 1) if h + 1 < GROUP else None
        total, summed = 0.0, 0.0
        for b, block in enumerate(blocks):
            weights = jnp.exp2(scores[b] * SCALE - (peak + hidden[b]))
            total = total + jnp.sum(weights, axis=0, keepdims=True)
            summed = summed + lax.dot_general(
                block[span : 2 * span, :],
                weights.astype(jnp.bfloat16),
                (((0,), (0,)), ((), ())),
                preferred_element_type=jnp.float32,
            )
        attended[:, h * HD : (h + 1) * HD] = jnp.transpose(summed * (1.0 / total)).astype(jnp.bfloat16)
    out_copies = []
    for j in range(parts):
        w_copies[j].wait()
        out_ref[j] = jnp.dot(attended[...], w_ref[j], preferred_element_type=jnp.float32).astype(jnp.bfloat16)
        out_copies.append(pltpu.make_async_copy(out_ref.at[j], out_hbm.at[j], out_sem.at[j]))
        out_copies[j].start()
    for copy in out_copies:
        copy.wait()


def routes(masks, spans):
    low, middle, high = in_order(masks)
    shift = (spans // 4).bit_length() - 1

    def after(mask, held):
        quarter = mask >> shift
        beside = (quarter == (held >> shift)) & (quarter > 0) & (quarter < 3)
        return jnp.where(beside, spans + jnp.bitwise_xor(mask, held), mask)

    return low, after(middle, low), after(high, middle)


def prepare(spans, masks_ref, key_ref, value_ref, kv_ref, low_ref, middle_ref, high_ref):
    span = key_ref.shape[0]
    low_ref[0], middle_ref[0], high_ref[0] = routes(masks_ref, spans)
    kv_ref[0:span, :] = key_ref[...]
    kv_ref[span:, :] = value_ref[...]


def across_chips(block, mask):
    if mask == 0:
        return block
    return lax.ppermute(block, "chip", [(i, i ^ mask) for i in range(lax.axis_size("chip"))])


def across_cores(block):
    return lax.ppermute(block, "core", [(0, 1), (1, 0)])


def direct(mask):
    return lambda own, other, *_: across_chips(other if mask & 1 else own, mask >> 1)


def onward(block, rest):
    return across_chips(across_cores(block) if rest & 1 else block, rest >> 1)


def by_mirror(rest):
    return lambda own, other, mirrored, *_: onward(mirrored, rest)


def by_held(rest):
    return lambda own, other, mirrored, held: onward(held, rest)


def nearer(mask, spans):
    if mask & 1:
        return mask >= spans * 11 // 16 or spans // 2 <= mask < spans * 5 // 8
    return mask >= spans * 7 // 8


def fetch(kv, low, middle, high):
    spans = 2 * lax.axis_size("chip")
    last = spans - 1
    mirrored = lax.ppermute(kv, ("chip", "core"), [(i, i ^ last) for i in range(spans)])
    other = across_cores(kv)
    plain = [direct(k) for k in range(spans)]
    mixed = [by_mirror(k ^ last) if nearer(k, spans) else direct(k) for k in range(spans)]
    mixed += [by_held(k) for k in range(spans // 4)]
    first = lax.switch(low, plain, kv, other)
    second = lax.switch(middle, mixed, kv, other, mirrored, first)
    third = lax.switch(high, mixed, kv, other, mirrored, second)
    return mirrored, first, second, third


def per_device(query_rows, key_rows, value_rows, out_weight, span_starts, round_masks):
    span, width = query_rows.shape
    heads = lax.axis_size("head")
    cut = out_weight.shape[1] // heads
    vmem = pl.BlockSpec(memory_space=pltpu.VMEM)
    smem = pl.BlockSpec(memory_space=pltpu.SMEM)
    anywhere = pl.BlockSpec(memory_space=pl.ANY)
    scalar = jax.ShapeDtypeStruct((1,), jnp.int32)
    kv, low, middle, high = pl.pallas_call(
        functools.partial(prepare, 2 * lax.axis_size("chip")),
        in_specs=[smem, vmem, vmem],
        out_specs=[vmem, smem, smem, smem],
        out_shape=[jax.ShapeDtypeStruct((2 * span, HD), jnp.bfloat16), scalar, scalar, scalar],
        name="prepare",
    )(round_masks, key_rows, value_rows)
    fars = fetch(kv, low[0], middle[0], high[0])
    shares = pl.pallas_call(
        attend_project,
        in_specs=[smem] * 2 + [vmem] * 6 + [anywhere],
        out_specs=anywhere,
        out_shape=jax.ShapeDtypeStruct((heads, span, cut), jnp.bfloat16),
        scratch_shapes=[
            pltpu.VMEM((span, width), jnp.bfloat16),
            pltpu.VMEM((heads, width, cut), jnp.bfloat16),
            pltpu.VMEM((heads, span, cut), jnp.bfloat16),
            pltpu.SemaphoreType.DMA((heads,)),
            pltpu.SemaphoreType.DMA((heads,)),
        ],
        compiler_params=pltpu.CompilerParams(vmem_limit_bytes=56 * 2**20),
        cost_estimate=pl.CostEstimate(flops=3 * 2**30, bytes_accessed=8 * 2**20, transcendentals=2**21),
        name="attend_project",
    )(span_starts, round_masks, query_rows, kv, *fars, out_weight)
    got = lax.all_to_all(shares, "head", 0, 0, tiled=True)
    return jnp.sum(got.astype(jnp.float32), axis=0).astype(jnp.bfloat16)


def solution(mesh):
    seq, head = mesh.devices.shape
    fine = Mesh(mesh.devices.reshape(seq // 2, 2, head), ("chip", "core", "head"))
    rows = ("chip", "core")
    in_specs = (P(rows, "head"), P(rows, "head"), P(rows, "head"), P("head", None), P(), P())
    return jax.shard_map(
        per_device, mesh=fine, in_specs=in_specs, out_specs=P(rows, "head"), check_vma=False
    )
```

```python
import functools

import jax
import jax.numpy as jnp
from jax import lax
from jax.experimental import pallas as pl
from jax.experimental.pallas import tpu as pltpu
from jax.sharding import Mesh, PartitionSpec as P

HD = 128
GROUP = 4
FAR_BELOW = -1e30
SCALE = HD ** (-0.5) * 1.4426950408889634


def in_order(masks, spans):
    def turned(mask):
        return jnp.where(mask < spans // 2, jnp.bitwise_xor(mask, spans // 4), mask)

    a, b, c = turned(masks[1]), turned(masks[2]), turned(masks[3])
    low = jnp.minimum(jnp.minimum(a, b), c)
    high = jnp.maximum(jnp.maximum(a, b), c)
    return turned(low), turned(a + b + c - low - high), turned(high)


def attend_project(
    starts_ref, masks_ref, q_ref, kv_ref, f0, f1, f2, f3, w_hbm, out_hbm, attended, w_ref, out_ref, w_sem, out_sem
):
    span = q_ref.shape[0]
    parts, _, cut = out_ref.shape
    w_copies = [
        pltpu.make_async_copy(w_hbm.at[:, pl.ds(j * cut, cut)], w_ref.at[j], w_sem.at[j]) for j in range(parts)
    ]
    for copy in w_copies:
        copy.start()
    me = lax.axis_index(("chip", "core"))
    own_start = starts_ref[me]
    blocks = [kv_ref, f0, f1, f2, f3]
    hidden = [0.0]
    for mask in (masks_ref[0], *in_order(masks_ref, starts_ref.shape[0])):
        partner = jnp.bitwise_xor(me, mask)
        hidden.append(jnp.where(starts_ref[partner] < own_start, 0.0, -FAR_BELOW))
    key = lax.broadcasted_iota(jnp.int32, (span, span), 0)
    token = lax.broadcasted_iota(jnp.int32, (span, span), 1)

    def score(h):
        q = q_ref[:, h * HD : (h + 1) * HD]
        scores, peak = [], None
        for b, block in enumerate(blocks):
            part = lax.dot_general(
                block[0:span, :], q, (((1,), (1,)), ((), ())), preferred_element_type=jnp.float32
            )
            if b == 0:
                part = jnp.where(key <= token, part, FAR_BELOW)
            part_peak = jnp.max(part, axis=0, keepdims=True) * SCALE - hidden[b]
            peak = part_peak if b == 0 else jnp.maximum(peak, part_peak)
            scores.append(part)
        return scores, peak

    ahead = score(0)
    for h in range(GROUP):
        scores, peak = ahead
        ahead = score(h + 1) if h + 1 < GROUP else None
        total, summed = 0.0, 0.0
        for b, block in enumerate(blocks):
            weights = jnp.exp2(scores[b] * SCALE - (peak + hidden[b]))
            total = total + jnp.sum(weights, axis=0, keepdims=True)
            summed = summed + lax.dot_general(
                block[span : 2 * span, :],
                weights.astype(jnp.bfloat16),
                (((0,), (0,)), ((), ())),
                preferred_element_type=jnp.float32,
            )
        attended[:, h * HD : (h + 1) * HD] = jnp.transpose(summed * (1.0 / total)).astype(jnp.bfloat16)
    out_copies = []
    for j in range(parts):
        w_copies[j].wait()
        out_ref[j] = jnp.dot(attended[...], w_ref[j], preferred_element_type=jnp.float32).astype(jnp.bfloat16)
        out_copies.append(pltpu.make_async_copy(out_ref.at[j], out_hbm.at[j], out_sem.at[j]))
        out_copies[j].start()
    for copy in out_copies:
        copy.wait()


def routes(masks, spans):
    low, middle, high = in_order(masks, spans)
    part = spans // 4
    shift = part.bit_length() - 1

    def after(mask, held):
        rest = jnp.bitwise_xor(mask, held)
        quarter = mask >> shift
        same = (quarter == (held >> shift)) & (quarter > 0) & (quarter < 3)
        across = (quarter == 2) & ((held >> shift) == 1) & ((rest & 1) == 0)
        return jnp.where(same, spans + rest, jnp.where(across, 2 * part + rest, mask))

    return low, after(middle, low), after(high, middle)


def prepare(spans, masks_ref, key_ref, value_ref, kv_ref, low_ref, middle_ref, high_ref):
    span = key_ref.shape[0]
    low_ref[0], middle_ref[0], high_ref[0] = routes(masks_ref, spans)
    kv_ref[0:span, :] = key_ref[...]
    kv_ref[span:, :] = value_ref[...]


def across_chips(block, mask):
    if mask == 0:
        return block
    return lax.ppermute(block, "chip", [(i, i ^ mask) for i in range(lax.axis_size("chip"))])


def across_cores(block):
    return lax.ppermute(block, "core", [(0, 1), (1, 0)])


def direct(mask):
    return lambda own, other, *_: across_chips(other if mask & 1 else own, mask >> 1)


def onward(block, rest):
    return across_chips(across_cores(block) if rest & 1 else block, rest >> 1)


def by_mirror(rest):
    return lambda own, other, mirrored, *_: onward(mirrored, rest)


def by_held(rest):
    return lambda own, other, mirrored, held: onward(held, rest)


def nearer(mask, spans):
    if mask & 1:
        return mask >= spans * 11 // 16 or spans // 2 <= mask < spans * 5 // 8
    return mask >= spans * 7 // 8


def fetch(kv, low, middle, high):
    spans = 2 * lax.axis_size("chip")
    last = spans - 1
    mirrored = lax.ppermute(kv, ("chip", "core"), [(i, i ^ last) for i in range(spans)])
    other = across_cores(kv)
    plain = [direct(k) for k in range(spans)]
    mixed = [by_mirror(k ^ last) if nearer(k, spans) else direct(k) for k in range(spans)]
    mixed += [by_held(k) for k in range(spans // 4)]
    mixed += [by_held(k) for k in range(spans * 3 // 4, spans)]
    first = lax.switch(low, plain, kv, other)
    second = lax.switch(middle, mixed, kv, other, mirrored, first)
    third = lax.switch(high, mixed, kv, other, mirrored, second)
    return mirrored, first, second, third


def per_device(query_rows, key_rows, value_rows, out_weight, span_starts, round_masks):
    span, width = query_rows.shape
    heads = lax.axis_size("head")
    cut = out_weight.shape[1] // heads
    vmem = pl.BlockSpec(memory_space=pltpu.VMEM)
    smem = pl.BlockSpec(memory_space=pltpu.SMEM)
    anywhere = pl.BlockSpec(memory_space=pl.ANY)
    scalar = jax.ShapeDtypeStruct((1,), jnp.int32)
    kv, low, middle, high = pl.pallas_call(
        functools.partial(prepare, 2 * lax.axis_size("chip")),
        in_specs=[smem, vmem, vmem],
        out_specs=[vmem, smem, smem, smem],
        out_shape=[jax.ShapeDtypeStruct((2 * span, HD), jnp.bfloat16), scalar, scalar, scalar],
        name="prepare",
    )(round_masks, key_rows, value_rows)
    fars = fetch(kv, low[0], middle[0], high[0])
    shares = pl.pallas_call(
        attend_project,
        in_specs=[smem] * 2 + [vmem] * 6 + [anywhere],
        out_specs=anywhere,
        out_shape=jax.ShapeDtypeStruct((heads, span, cut), jnp.bfloat16),
        scratch_shapes=[
            pltpu.VMEM((span, width), jnp.bfloat16),
            pltpu.VMEM((heads, width, cut), jnp.bfloat16),
            pltpu.VMEM((heads, span, cut), jnp.bfloat16),
            pltpu.SemaphoreType.DMA((heads,)),
            pltpu.SemaphoreType.DMA((heads,)),
        ],
        compiler_params=pltpu.CompilerParams(vmem_limit_bytes=56 * 2**20),
        cost_estimate=pl.CostEstimate(flops=3 * 2**30, bytes_accessed=8 * 2**20, transcendentals=2**21),
        name="attend_project",
    )(span_starts, round_masks, query_rows, kv, *fars, out_weight)
    got = lax.all_to_all(shares, "head", 0, 0, tiled=True)
    return jnp.sum(got.astype(jnp.float32), axis=0).astype(jnp.bfloat16)


def solution(mesh):
    seq, head = mesh.devices.shape
    fine = Mesh(mesh.devices.reshape(seq // 2, 2, head), ("chip", "core", "head"))
    rows = ("chip", "core")
    in_specs = (P(rows, "head"), P(rows, "head"), P(rows, "head"), P("head", None), P(), P())
    return jax.shard_map(
        per_device, mesh=fine, in_specs=in_specs, out_specs=P(rows, "head"), check_vma=False
    )
```

```python
import functools

import jax
import jax.numpy as jnp
from jax import lax
from jax.experimental import pallas as pl
from jax.experimental.pallas import tpu as pltpu
from jax.sharding import Mesh, PartitionSpec as P

HD = 128
GROUP = 4
FAR_BELOW = -1e30
SCALE = HD ** (-0.5) * 1.4426950408889634


def in_order(masks, spans):
    part = spans // 4

    def place(mask):
        return jnp.where(mask < part, mask + 2 * part, jnp.where(mask < 3 * part, mask - part, mask))

    def at(place):
        return jnp.where(place < 2 * part, place + part, jnp.where(place < 3 * part, place - 2 * part, place))

    a, b, c = place(masks[1]), place(masks[2]), place(masks[3])
    low = jnp.minimum(jnp.minimum(a, b), c)
    high = jnp.maximum(jnp.maximum(a, b), c)
    return at(low), at(a + b + c - low - high), at(high)


def attend_project(
    starts_ref, masks_ref, q_ref, kv_ref, f0, f1, f2, f3, w_hbm, out_hbm, attended, w_ref, out_ref, w_sem, out_sem
):
    span = q_ref.shape[0]
    parts, _, cut = out_ref.shape
    w_copies = [
        pltpu.make_async_copy(w_hbm.at[:, pl.ds(j * cut, cut)], w_ref.at[j], w_sem.at[j]) for j in range(parts)
    ]
    for copy in w_copies:
        copy.start()
    me = lax.axis_index(("chip", "core"))
    own_start = starts_ref[me]
    blocks = [kv_ref, f0, f1, f2, f3]
    hidden = [0.0]
    for mask in (masks_ref[0], *in_order(masks_ref, starts_ref.shape[0])):
        partner = jnp.bitwise_xor(me, mask)
        hidden.append(jnp.where(starts_ref[partner] < own_start, 0.0, -FAR_BELOW))
    key = lax.broadcasted_iota(jnp.int32, (span, span), 0)
    token = lax.broadcasted_iota(jnp.int32, (span, span), 1)

    def score(h):
        q = q_ref[:, h * HD : (h + 1) * HD]
        scores, peak = [], None
        for b, block in enumerate(blocks):
            part = lax.dot_general(
                block[0:span, :], q, (((1,), (1,)), ((), ())), preferred_element_type=jnp.float32
            )
            if b == 0:
                part = jnp.where(key <= token, part, FAR_BELOW)
            part_peak = jnp.max(part, axis=0, keepdims=True) * SCALE - hidden[b]
            peak = part_peak if b == 0 else jnp.maximum(peak, part_peak)
            scores.append(part)
        return scores, peak

    ahead = score(0)
    for h in range(GROUP):
        scores, peak = ahead
        ahead = score(h + 1) if h + 1 < GROUP else None
        total, summed = 0.0, 0.0
        for b, block in enumerate(blocks):
            weights = jnp.exp2(scores[b] * SCALE - (peak + hidden[b]))
            total = total + jnp.sum(weights, axis=0, keepdims=True)
            summed = summed + lax.dot_general(
                block[span : 2 * span, :],
                weights.astype(jnp.bfloat16),
                (((0,), (0,)), ((), ())),
                preferred_element_type=jnp.float32,
            )
        attended[:, h * HD : (h + 1) * HD] = jnp.transpose(summed * (1.0 / total)).astype(jnp.bfloat16)
    out_copies = []
    for j in range(parts):
        w_copies[j].wait()
        out_ref[j] = jnp.dot(attended[...], w_ref[j], preferred_element_type=jnp.float32).astype(jnp.bfloat16)
        out_copies.append(pltpu.make_async_copy(out_ref.at[j], out_hbm.at[j], out_sem.at[j]))
        out_copies[j].start()
    for copy in out_copies:
        copy.wait()


def routes(masks, spans):
    low, middle, high = in_order(masks, spans)
    shift = (spans // 4).bit_length() - 1

    def after(mask, held):
        rest = jnp.bitwise_xor(mask, held)
        quarter = mask >> shift
        same = (quarter == (held >> shift)) & (quarter > 0) & (quarter < 3)
        return jnp.where(same, spans + rest, mask)

    return low, after(middle, low), after(high, middle)


def prepare(spans, masks_ref, key_ref, value_ref, kv_ref, low_ref, middle_ref, high_ref):
    span = key_ref.shape[0]
    low_ref[0], middle_ref[0], high_ref[0] = routes(masks_ref, spans)
    kv_ref[0:span, :] = key_ref[...]
    kv_ref[span:, :] = value_ref[...]


def across_chips(block, mask):
    if mask == 0:
        return block
    return lax.ppermute(block, "chip", [(i, i ^ mask) for i in range(lax.axis_size("chip"))])


def across_cores(block):
    return lax.ppermute(block, "core", [(0, 1), (1, 0)])


def direct(mask):
    return lambda own, other, *_: across_chips(other if mask & 1 else own, mask >> 1)


def onward(block, rest):
    return across_chips(across_cores(block) if rest & 1 else block, rest >> 1)


def by_mirror(rest):
    return lambda own, other, mirrored, *_: onward(mirrored, rest)


def by_held(rest):
    return lambda own, other, mirrored, held: onward(held, rest)


def nearer(mask, spans):
    if mask & 1:
        return mask >= spans * 11 // 16 or spans // 2 <= mask < spans * 5 // 8
    return mask >= spans * 7 // 8


def fetch(kv, low, middle, high):
    spans = 2 * lax.axis_size("chip")
    last = spans - 1
    mirrored = lax.ppermute(kv, ("chip", "core"), [(i, i ^ last) for i in range(spans)])
    other = across_cores(kv)
    plain = [direct(k) for k in range(spans)]
    mixed = [by_mirror(k ^ last) if nearer(k, spans) else direct(k) for k in range(spans)]
    mixed += [by_held(k) for k in range(spans // 4)]
    first = lax.switch(low, plain, kv, other)
    second = lax.switch(middle, mixed, kv, other, mirrored, first)
    third = lax.switch(high, mixed, kv, other, mirrored, second)
    return mirrored, first, second, third


def per_device(query_rows, key_rows, value_rows, out_weight, span_starts, round_masks):
    span, width = query_rows.shape
    heads = lax.axis_size("head")
    cut = out_weight.shape[1] // heads
    vmem = pl.BlockSpec(memory_space=pltpu.VMEM)
    smem = pl.BlockSpec(memory_space=pltpu.SMEM)
    anywhere = pl.BlockSpec(memory_space=pl.ANY)
    scalar = jax.ShapeDtypeStruct((1,), jnp.int32)
    kv, low, middle, high = pl.pallas_call(
        functools.partial(prepare, 2 * lax.axis_size("chip")),
        in_specs=[smem, vmem, vmem],
        out_specs=[vmem, smem, smem, smem],
        out_shape=[jax.ShapeDtypeStruct((2 * span, HD), jnp.bfloat16), scalar, scalar, scalar],
        name="prepare",
    )(round_masks, key_rows, value_rows)
    fars = fetch(kv, low[0], middle[0], high[0])
    shares = pl.pallas_call(
        attend_project,
        in_specs=[smem] * 2 + [vmem] * 6 + [anywhere],
        out_specs=anywhere,
        out_shape=jax.ShapeDtypeStruct((heads, span, cut), jnp.bfloat16),
        scratch_shapes=[
            pltpu.VMEM((span, width), jnp.bfloat16),
            pltpu.VMEM((heads, width, cut), jnp.bfloat16),
            pltpu.VMEM((heads, span, cut), jnp.bfloat16),
            pltpu.SemaphoreType.DMA((heads,)),
            pltpu.SemaphoreType.DMA((heads,)),
        ],
        compiler_params=pltpu.CompilerParams(vmem_limit_bytes=56 * 2**20),
        cost_estimate=pl.CostEstimate(flops=3 * 2**30, bytes_accessed=8 * 2**20, transcendentals=2**21),
        name="attend_project",
    )(span_starts, round_masks, query_rows, kv, *fars, out_weight)
    got = lax.all_to_all(shares, "head", 0, 0, tiled=True)
    return jnp.sum(got.astype(jnp.float32), axis=0).astype(jnp.bfloat16)


def solution(mesh):
    seq, head = mesh.devices.shape
    fine = Mesh(mesh.devices.reshape(seq // 2, 2, head), ("chip", "core", "head"))
    rows = ("chip", "core")
    in_specs = (P(rows, "head"), P(rows, "head"), P(rows, "head"), P("head", None), P(), P())
    return jax.shard_map(
        per_device, mesh=fine, in_specs=in_specs, out_specs=P(rows, "head"), check_vma=False
    )
```

```python
import functools

import jax
import jax.numpy as jnp
from jax import lax
from jax.experimental import pallas as pl
from jax.experimental.pallas import tpu as pltpu
from jax.sharding import Mesh, PartitionSpec as P

HD = 128
GROUP = 4
FAR_BELOW = -1e30
SCALE = HD ** (-0.5) * 1.4426950408889634


def in_order(masks, spans):
    part = spans // 4

    def place(mask):
        return jnp.where(mask < part, mask + 2 * part, jnp.where(mask < 3 * part, mask - part, mask))

    def at(place):
        return jnp.where(place < 2 * part, place + part, jnp.where(place < 3 * part, place - 2 * part, place))

    a, b, c = place(masks[1]), place(masks[2]), place(masks[3])
    low = jnp.minimum(jnp.minimum(a, b), c)
    high = jnp.maximum(jnp.maximum(a, b), c)
    return at(low), at(a + b + c - low - high), at(high)


def attend_project(
    starts_ref, masks_ref, q_ref, kv_ref, f0, f1, f2, f3, w_hbm, out_hbm, attended, w_ref, out_ref, w_sem, out_sem
):
    span = q_ref.shape[0]
    parts, _, cut = out_ref.shape
    w_copy = pltpu.make_async_copy(w_hbm, w_ref, w_sem)
    w_copy.start()
    me = lax.axis_index(("chip", "core"))
    own_start = starts_ref[me]
    blocks = [kv_ref, f0, f1, f2, f3]
    hidden = [0.0]
    for mask in (masks_ref[0], *in_order(masks_ref, starts_ref.shape[0])):
        partner = jnp.bitwise_xor(me, mask)
        hidden.append(jnp.where(starts_ref[partner] < own_start, 0.0, -FAR_BELOW))
    key = lax.broadcasted_iota(jnp.int32, (span, span), 0)
    token = lax.broadcasted_iota(jnp.int32, (span, span), 1)

    def score(h):
        q = q_ref[:, h * HD : (h + 1) * HD]
        scores, peak = [], None
        for b, block in enumerate(blocks):
            part = lax.dot_general(
                block[0:span, :], q, (((1,), (1,)), ((), ())), preferred_element_type=jnp.float32
            )
            if b == 0:
                part = jnp.where(key <= token, part, FAR_BELOW)
            part_peak = jnp.max(part, axis=0, keepdims=True) * SCALE - hidden[b]
            peak = part_peak if b == 0 else jnp.maximum(peak, part_peak)
            scores.append(part)
        return scores, peak

    ahead = score(0)
    for h in range(GROUP):
        scores, peak = ahead
        ahead = score(h + 1) if h + 1 < GROUP else None
        total, summed = 0.0, 0.0
        for b, block in enumerate(blocks):
            weights = jnp.exp2(scores[b] * SCALE - (peak + hidden[b]))
            total = total + jnp.sum(weights, axis=0, keepdims=True)
            summed = summed + lax.dot_general(
                block[span : 2 * span, :],
                weights.astype(jnp.bfloat16),
                (((0,), (0,)), ((), ())),
                preferred_element_type=jnp.float32,
            )
        attended[:, h * HD : (h + 1) * HD] = jnp.transpose(summed * (1.0 / total)).astype(jnp.bfloat16)
    out_copies = []
    w_copy.wait()
    for j in range(parts):
        out_ref[j] = jnp.dot(
            attended[...], w_ref[:, j * cut : (j + 1) * cut], preferred_element_type=jnp.float32
        ).astype(jnp.bfloat16)
        out_copies.append(pltpu.make_async_copy(out_ref.at[j], out_hbm.at[j], out_sem.at[j]))
        out_copies[j].start()
    for copy in out_copies:
        copy.wait()


def routes(masks, spans):
    low, middle, high = in_order(masks, spans)
    shift = (spans // 4).bit_length() - 1

    def after(mask, held):
        rest = jnp.bitwise_xor(mask, held)
        quarter = mask >> shift
        same = (quarter == (held >> shift)) & (quarter > 0) & (quarter < 3)
        return jnp.where(same, spans + rest, mask)

    return low, after(middle, low), after(high, middle)


def prepare(spans, masks_ref, key_ref, value_ref, kv_ref, low_ref, middle_ref, high_ref):
    span = key_ref.shape[0]
    low_ref[0], middle_ref[0], high_ref[0] = routes(masks_ref, spans)
    kv_ref[0:span, :] = key_ref[...]
    kv_ref[span:, :] = value_ref[...]


def across_chips(block, mask):
    if mask == 0:
        return block
    return lax.ppermute(block, "chip", [(i, i ^ mask) for i in range(lax.axis_size("chip"))])


def across_cores(block):
    return lax.ppermute(block, "core", [(0, 1), (1, 0)])


def direct(mask):
    return lambda own, other, *_: across_chips(other if mask & 1 else own, mask >> 1)


def onward(block, rest):
    return across_chips(across_cores(block) if rest & 1 else block, rest >> 1)


def by_mirror(rest):
    return lambda own, other, mirrored, *_: onward(mirrored, rest)


def by_held(rest):
    return lambda own, other, mirrored, held: onward(held, rest)


def nearer(mask, spans):
    if mask & 1:
        return mask >= spans * 11 // 16 or spans // 2 <= mask < spans * 5 // 8
    return mask >= spans * 7 // 8


def fetch(kv, low, middle, high):
    spans = 2 * lax.axis_size("chip")
    last = spans - 1
    mirrored = lax.ppermute(kv, ("chip", "core"), [(i, i ^ last) for i in range(spans)])
    other = across_cores(kv)
    plain = [direct(k) for k in range(spans)]
    mixed = [by_mirror(k ^ last) if nearer(k, spans) else direct(k) for k in range(spans)]
    mixed += [by_held(k) for k in range(spans // 4)]
    first = lax.switch(low, plain, kv, other)
    second = lax.switch(middle, mixed, kv, other, mirrored, first)
    third = lax.switch(high, mixed, kv, other, mirrored, second)
    return mirrored, first, second, third


def per_device(query_rows, key_rows, value_rows, out_weight, span_starts, round_masks):
    span, width = query_rows.shape
    heads = lax.axis_size("head")
    cut = out_weight.shape[1] // heads
    vmem = pl.BlockSpec(memory_space=pltpu.VMEM)
    smem = pl.BlockSpec(memory_space=pltpu.SMEM)
    anywhere = pl.BlockSpec(memory_space=pl.ANY)
    scalar = jax.ShapeDtypeStruct((1,), jnp.int32)
    kv, low, middle, high = pl.pallas_call(
        functools.partial(prepare, 2 * lax.axis_size("chip")),
        in_specs=[smem, vmem, vmem],
        out_specs=[vmem, smem, smem, smem],
        out_shape=[jax.ShapeDtypeStruct((2 * span, HD), jnp.bfloat16), scalar, scalar, scalar],
        name="prepare",
    )(round_masks, key_rows, value_rows)
    fars = fetch(kv, low[0], middle[0], high[0])
    shares = pl.pallas_call(
        attend_project,
        in_specs=[smem] * 2 + [vmem] * 6 + [anywhere],
        out_specs=anywhere,
        out_shape=jax.ShapeDtypeStruct((heads, span, cut), jnp.bfloat16),
        scratch_shapes=[
            pltpu.VMEM((span, width), jnp.bfloat16),
            pltpu.VMEM((width, heads * cut), jnp.bfloat16),
            pltpu.VMEM((heads, span, cut), jnp.bfloat16),
            pltpu.SemaphoreType.DMA,
            pltpu.SemaphoreType.DMA((heads,)),
        ],
        compiler_params=pltpu.CompilerParams(vmem_limit_bytes=56 * 2**20),
        cost_estimate=pl.CostEstimate(flops=3 * 2**30, bytes_accessed=8 * 2**20, transcendentals=2**21),
        name="attend_project",
    )(span_starts, round_masks, query_rows, kv, *fars, out_weight)
    got = lax.all_to_all(shares, "head", 0, 0, tiled=True)
    return jnp.sum(got.astype(jnp.float32), axis=0).astype(jnp.bfloat16)


def solution(mesh):
    seq, head = mesh.devices.shape
    fine = Mesh(mesh.devices.reshape(seq // 2, 2, head), ("chip", "core", "head"))
    rows = ("chip", "core")
    in_specs = (P(rows, "head"), P(rows, "head"), P(rows, "head"), P("head", None), P(), P())
    return jax.shard_map(
        per_device, mesh=fine, in_specs=in_specs, out_specs=P(rows, "head"), check_vma=False
    )
```

```python
import functools

import jax
import jax.numpy as jnp
from jax import lax
from jax.experimental import pallas as pl
from jax.experimental.pallas import tpu as pltpu
from jax.sharding import Mesh, PartitionSpec as P

HD = 128
GROUP = 4
FAR_BELOW = -1e30
SCALE = HD ** (-0.5) * 1.4426950408889634


def in_order(masks, spans):
    part = spans // 4

    def place(mask):
        return jnp.where(mask < part, mask + 2 * part, jnp.where(mask < 3 * part, mask - part, mask))

    def at(place):
        return jnp.where(place < 2 * part, place + part, jnp.where(place < 3 * part, place - 2 * part, place))

    a, b, c = place(masks[1]), place(masks[2]), place(masks[3])
    low = jnp.minimum(jnp.minimum(a, b), c)
    high = jnp.maximum(jnp.maximum(a, b), c)
    return at(low), at(a + b + c - low - high), at(high)


def attend_project(
    starts_ref, masks_ref, q_ref, kv_ref, f0, f1, f2, f3, w_hbm, out_hbm, attended, w_ref, out_ref, w_sem, out_sem
):
    span = q_ref.shape[0]
    parts, _, cut = out_ref.shape
    w_copies = [
        pltpu.make_async_copy(w_hbm.at[:, pl.ds(j * cut, cut)], w_ref.at[j], w_sem.at[j]) for j in range(parts)
    ]
    for copy in w_copies:
        copy.start()
    me = lax.axis_index(("chip", "core"))
    own_start = starts_ref[me]
    blocks = [kv_ref, f0, f1, f2, f3]
    hidden = [0.0]
    for mask in (masks_ref[0], *in_order(masks_ref, starts_ref.shape[0])):
        partner = jnp.bitwise_xor(me, mask)
        hidden.append(jnp.where(starts_ref[partner] < own_start, 0.0, -FAR_BELOW))
    key = lax.broadcasted_iota(jnp.int32, (span, span), 0)
    token = lax.broadcasted_iota(jnp.int32, (span, span), 1)

    def score(h):
        q = q_ref[:, h * HD : (h + 1) * HD]
        scores, peak = [], None
        for b, block in enumerate(blocks):
            part = lax.dot_general(
                block[0:span, :], q, (((1,), (1,)), ((), ())), preferred_element_type=jnp.float32
            )
            if b == 0:
                part = jnp.where(key <= token, part, FAR_BELOW)
            part_peak = jnp.max(part, axis=0, keepdims=True) * SCALE - hidden[b]
            peak = part_peak if b == 0 else jnp.maximum(peak, part_peak)
            scores.append(part)
        return scores, peak

    ahead = score(0)
    for h in range(GROUP):
        scores, peak = ahead
        ahead = score(h + 1) if h + 1 < GROUP else None
        total, summed = 0.0, 0.0
        for b, block in enumerate(blocks):
            weights = jnp.exp2(scores[b] * SCALE - (peak + hidden[b]))
            total = total + jnp.sum(weights, axis=0, keepdims=True)
            summed = summed + lax.dot_general(
                block[span : 2 * span, :],
                weights.astype(jnp.bfloat16),
                (((0,), (0,)), ((), ())),
                preferred_element_type=jnp.float32,
            )
        attended[:, h * HD : (h + 1) * HD] = jnp.transpose(summed * (1.0 / total)).astype(jnp.bfloat16)
    out_copies = []
    for j in range(parts):
        w_copies[j].wait()
        out_ref[j] = jnp.dot(attended[...], w_ref[j], preferred_element_type=jnp.float32).astype(jnp.bfloat16)
        out_copies.append(pltpu.make_async_copy(out_ref.at[j], out_hbm.at[j], out_sem.at[j]))
        out_copies[j].start()
    for copy in out_copies:
        copy.wait()


def routes(masks, spans):
    low, middle, high = in_order(masks, spans)
    shift = (spans // 4).bit_length() - 1

    def after(mask, held):
        rest = jnp.bitwise_xor(mask, held)
        quarter = mask >> shift
        same = (quarter == (held >> shift)) & (quarter > 0) & (quarter < 3)
        return jnp.where(same, spans + rest, mask)

    return low, after(middle, low), after(high, middle)


def prepare(spans, masks_ref, key_ref, value_ref, kv_ref, low_ref, middle_ref, high_ref):
    span = key_ref.shape[0]
    low_ref[0], middle_ref[0], high_ref[0] = routes(masks_ref, spans)
    kv_ref[0:span, :] = key_ref[...]
    kv_ref[span:, :] = value_ref[...]


def across_chips(block, mask):
    if mask == 0:
        return block
    return lax.ppermute(block, "chip", [(i, i ^ mask) for i in range(lax.axis_size("chip"))])


def across_cores(block):
    return lax.ppermute(block, "core", [(0, 1), (1, 0)])


def direct(mask):
    return lambda own, other, *_: across_chips(other if mask & 1 else own, mask >> 1)


def onward(block, rest):
    return across_chips(across_cores(block) if rest & 1 else block, rest >> 1)


def by_mirror(rest):
    return lambda own, other, mirrored, *_: onward(mirrored, rest)


def by_held(rest):
    return lambda own, other, mirrored, held: onward(held, rest)


def nearer(mask, spans):
    if mask & 1:
        return mask >= spans * 11 // 16 or spans // 2 <= mask < spans * 5 // 8
    return mask >= spans * 7 // 8 or spans // 2 <= mask < spans * 11 // 16


def fetch(kv, low, middle, high):
    spans = 2 * lax.axis_size("chip")
    last = spans - 1
    mirrored = lax.ppermute(kv, ("chip", "core"), [(i, i ^ last) for i in range(spans)])
    other = across_cores(kv)
    plain = [direct(k) for k in range(spans)]
    mixed = [by_mirror(k ^ last) if nearer(k, spans) else direct(k) for k in range(spans)]
    mixed += [by_held(k) for k in range(spans // 4)]
    first = lax.switch(low, plain, kv, other)
    second = lax.switch(middle, mixed, kv, other, mirrored, first)
    third = lax.switch(high, mixed, kv, other, mirrored, second)
    return mirrored, first, second, third


def per_device(query_rows, key_rows, value_rows, out_weight, span_starts, round_masks):
    span, width = query_rows.shape
    heads = lax.axis_size("head")
    cut = out_weight.shape[1] // heads
    vmem = pl.BlockSpec(memory_space=pltpu.VMEM)
    smem = pl.BlockSpec(memory_space=pltpu.SMEM)
    anywhere = pl.BlockSpec(memory_space=pl.ANY)
    scalar = jax.ShapeDtypeStruct((1,), jnp.int32)
    kv, low, middle, high = pl.pallas_call(
        functools.partial(prepare, 2 * lax.axis_size("chip")),
        in_specs=[smem, vmem, vmem],
        out_specs=[vmem, smem, smem, smem],
        out_shape=[jax.ShapeDtypeStruct((2 * span, HD), jnp.bfloat16), scalar, scalar, scalar],
        name="prepare",
    )(round_masks, key_rows, value_rows)
    fars = fetch(kv, low[0], middle[0], high[0])
    shares = pl.pallas_call(
        attend_project,
        in_specs=[smem] * 2 + [vmem] * 6 + [anywhere],
        out_specs=anywhere,
        out_shape=jax.ShapeDtypeStruct((heads, span, cut), jnp.bfloat16),
        scratch_shapes=[
            pltpu.VMEM((span, width), jnp.bfloat16),
            pltpu.VMEM((heads, width, cut), jnp.bfloat16),
            pltpu.VMEM((heads, span, cut), jnp.bfloat16),
            pltpu.SemaphoreType.DMA((heads,)),
            pltpu.SemaphoreType.DMA((heads,)),
        ],
        compiler_params=pltpu.CompilerParams(vmem_limit_bytes=56 * 2**20),
        cost_estimate=pl.CostEstimate(flops=3 * 2**30, bytes_accessed=8 * 2**20, transcendentals=2**21),
        name="attend_project",
    )(span_starts, round_masks, query_rows, kv, *fars, out_weight)
    got = lax.all_to_all(shares, "head", 0, 0, tiled=True)
    return jnp.sum(got.astype(jnp.float32), axis=0).astype(jnp.bfloat16)


def solution(mesh):
    seq, head = mesh.devices.shape
    fine = Mesh(mesh.devices.reshape(seq // 2, 2, head), ("chip", "core", "head"))
    rows = ("chip", "core")
    in_specs = (P(rows, "head"), P(rows, "head"), P(rows, "head"), P("head", None), P(), P())
    return jax.shard_map(
        per_device, mesh=fine, in_specs=in_specs, out_specs=P(rows, "head"), check_vma=False
    )
```
